32 devices in a mesh: ma: 4 (over z), row: 8 (over y, x, core).
Axes of the slice: x: 2, y: 2, z: 4, core: 2. Of those that a mesh axis runs over, the one named last changes fastest.
Arguments:
- spectra: float32 [8, 3, 256, 513, 2], P('row', None, 'ma'), may hold values from -0.3125 to 0.3125
- legendre: bfloat16 [256, 513, 384], P('ma'), may hold values from -0.25 to 0.25
- pair_slots: int32 [256], replicated, may hold values from 0 to 255, each once
- theta_owner: int32 [384], replicated, may hold values from 0 to 383, each once
Outputs:
- flux_grid: bfloat16 [8, 768, 2, 1536], P('row', 'ma')
- flux_spectra: float32 [8, 2, 256, 513, 2], P('row', None, 'ma')
The draws below stay inside these ranges and needn't reach their ends.
Inputs may be any that keep to these rules, and one draw needn't show every extreme that they name: `pair_slots`: A value p below 256 puts the orders p and 511 - p in that slot; values of 256 or more mark empty slots. `theta_owner`: index d of ma owns the northern rows at positions d * 96 to (d + 1) * 96 - 1 and their mirror rows.
All inputs are finite; a program needn't handle non-finite values.
Results may differ from the reference program's by a relative error of at most 0.0077.
Values may be sent and summed in bfloat16 or wider, within the bound.
A program may use at most 192 MiB of HBM per device.

```python
import jax
import jax.numpy as jnp
from jax import lax

LMAX = 511
NTHETA = 768
NPHI = 1536
NPAIRS = 256
PACK = 513
HALF = 384
SLOTS = 256
THETA_DEV = 192
LEVELS = 8
N_MA = 4


def block_scale(own_key, shape, split, low, largest):
    loudness = 1.0
    for position, blocks in split:
        heights = jax.random.uniform(jax.random.fold_in(jax.random.fold_in(own_key, 6), position), (blocks,), jnp.float32, low / len(split), largest / len(split))
        loudness = loudness * jnp.repeat(jnp.exp(heights), shape[position] // blocks).reshape((-1,) + (1,) * (len(shape) - 1 - position))
    return loudness


def noise(key, shape, scale, reach, cuts=(), held_as=jnp.bfloat16):
    level = block_scale(key, shape, cuts, -0.22, 0.18) if cuts else 1.0
    result = jax.random.normal(key, shape, jnp.float32) * scale * level
    return jnp.minimum(jnp.maximum(result, -reach), reach).astype(held_as)


def setup_inputs(seed: int = 0) -> dict:
    arg_keys = jax.random.split(jax.random.key(seed), 5)
    spectra = noise(arg_keys[0], (LEVELS, 3, SLOTS, PACK, 2), ((LEVELS * (LMAX + 1) // 2) ** -0.5), 0.3125, ((0, 8), (2, 4)), jnp.float32)
    legendre = noise(arg_keys[1], (SLOTS, PACK, HALF), PACK ** -0.5, 0.25, ((0, 4),))
    pair_slots = jax.random.permutation(arg_keys[2], SLOTS).astype(jnp.int32)
    theta_owner = jax.random.permutation(arg_keys[3], HALF).astype(jnp.int32)
    return {"spectra": spectra, "legendre": legendre, "pair_slots": pair_slots, "theta_owner": theta_owner}


HIGH = lax.Precision.HIGHEST


def chebyshev_pair(levels):
    index = jnp.arange(levels, dtype=jnp.int32)
    products = (index[:, None] * index[None, :]) % (2 * (levels - 1))
    cosines = jnp.cos(jnp.pi * products.astype(jnp.float32) / (levels - 1))
    ends = jnp.where((index == 0) | (index == levels - 1), 0.5, 1.0).astype(jnp.float32)
    analysis = (2.0 / (levels - 1)) ** 0.5 * ends[:, None] * ends[None, :] * cosines
    return cosines, analysis


def slot_tables(pairs):
    packed = jnp.arange(PACK, dtype=jnp.int32)[None, :]
    column = pairs[:, None]
    in_use = column < NPAIRS
    low_part = in_use & (packed <= LMAX - column)
    high_part = in_use & (packed > LMAX - column)
    high_sign = 1 - 2 * ((packed + LMAX - column + 1) % 2)
    low_sign = jnp.broadcast_to(1 - 2 * (packed % 2), high_sign.shape)
    slot_masks = jnp.stack([low_part, high_part]).astype(jnp.float32)
    slot_signs = jnp.stack([low_sign, high_sign])
    even_part = slot_masks * (slot_signs > 0)
    odd_part = slot_masks * (slot_signs < 0)
    select = jnp.stack([even_part, odd_part], axis=1)
    orders = jnp.stack([pairs, LMAX - pairs], axis=1)
    return select, orders


def fourier_tables(orders):
    points = jnp.arange(NPHI, dtype=jnp.int32)
    phase = (orders[:, :, None] * points[None, None, :]) % NPHI
    angles = 2.0 * jnp.pi * phase.astype(jnp.float32) / NPHI
    weight = jnp.where(orders == 0, 1.0, 2.0).astype(jnp.float32)[:, :, None]
    synth_tab = jnp.stack([weight * jnp.cos(angles), -weight * jnp.sin(angles)]).astype(jnp.bfloat16)
    analysis_tab = jnp.stack([jnp.cos(angles), -jnp.sin(angles)]).astype(jnp.bfloat16)
    return synth_tab, analysis_tab


def reference(spectra, legendre, pair_slots, theta_owner):
    synth_mat, analysis_mat = chebyshev_pair(LEVELS)
    level_sums = jnp.einsum("kn,nfsjc->kfsjc", synth_mat, spectra, precision=HIGH)
    level_coeffs = level_sums.astype(jnp.bfloat16)
    select, orders = slot_tables(pair_slots)
    synth_tab, analysis_tab = fourier_tables(orders)
    synth_wide = synth_tab.astype(jnp.float32)
    analysis_wide = analysis_tab.astype(jnp.float32)
    table_wide = legendre.astype(jnp.float32)
    own_half = THETA_DEV // 2

    def to_owner(values):
        return values[..., theta_owner].reshape(values.shape[:-1] + (N_MA, own_half))

    def level_pass(coeffs):
        halves = jnp.einsum("fsjc,vesj,sji->fcsvei", coeffs.astype(jnp.float32), select, table_wide, precision=HIGH)
        north_rows = (halves[:, :, :, :, 0] + halves[:, :, :, :, 1]).astype(jnp.bfloat16)
        south_rows = (halves[:, :, :, :, 0] - halves[:, :, :, :, 1]).astype(jnp.bfloat16)
        rows = jnp.stack([to_owner(north_rows), to_owner(south_rows)], axis=-2)
        rows = rows.reshape(north_rows.shape[:-1] + (NTHETA,))
        grid_vals = jnp.einsum("fcsvt,csvp->ftp", rows.astype(jnp.float32), synth_wide, precision=HIGH)
        flux_vals = (grid_vals[0:1] * grid_vals[1:3]).astype(jnp.bfloat16)
        fourier = jnp.einsum("gtp,csvp->gcsvt", flux_vals.astype(jnp.float32), analysis_wide, precision=HIGH) * NPHI ** -0.5
        split_rows = fourier.reshape(fourier.shape[:-1] + (N_MA, 2, own_half))
        north_own = split_rows[..., 0, :].reshape(fourier.shape[:-1] + (HALF,))
        south_own = split_rows[..., 1, :].reshape(fourier.shape[:-1] + (HALF,))
        base = jnp.zeros(fourier.shape[:-1] + (HALF,), jnp.float32)
        north_nat = base.at[..., theta_owner].set(north_own)
        south_nat = base.at[..., theta_owner].set(south_own)
        parity_sums = jnp.stack([north_nat + south_nat, north_nat - south_nat])
        spectral = jnp.einsum("egcsvi,sji,vesj->gsjc", parity_sums, table_wide, select, precision=HIGH)
        return jnp.transpose(flux_vals, (1, 0, 2)), spectral

    flux_grid, spectral = lax.map(level_pass, level_coeffs)
    flux_spectra = jnp.einsum("nk,kgsjc->ngsjc", analysis_mat, spectral, precision=HIGH)
    return flux_grid, flux_spectra
```

```python
import jax
import jax.numpy as jnp
from jax import lax
from jax.sharding import PartitionSpec as P

LMAX = 511
NPHI = 1536
NPAIRS = 256
PACK = 513
LANES = 128

HIGH = lax.Precision.HIGHEST
BF16 = jnp.bfloat16
F32 = jnp.float32


def chebyshev_pair(levels):
    index = jnp.arange(levels, dtype=jnp.int32)
    products = index[:, None] * index[None, :] % (2 * (levels - 1))
    cosines = jnp.cos(jnp.pi * products.astype(F32) / (levels - 1))
    ends = jnp.where((index == 0) | (index == levels - 1), 0.5, 1.0).astype(F32)
    analysis = (2.0 / (levels - 1)) ** 0.5 * ends[:, None] * ends[None, :] * cosines
    return (cosines, analysis)


def slot_weights(pairs):
    packed = jnp.arange(PACK, dtype=jnp.int32)[None, :]
    column = pairs[:, None]
    in_use = column < NPAIRS
    low = (in_use & (packed <= LMAX - column)).astype(F32)
    high = (in_use & (packed > LMAX - column)).astype(F32)
    low_sign = (1 - 2 * (packed % 2)).astype(F32)
    high_sign = (1 - 2 * ((packed + LMAX - column + 1) % 2)).astype(F32)
    return jnp.stack(
        [jnp.stack([low, low * low_sign], 1), jnp.stack([high, high * high_sign], 1)], 1
    )


def fourier_table(orders):
    points = jnp.arange(NPHI, dtype=jnp.int32)
    phase = orders[:, None, :, None] * points % NPHI
    angles = 2.0 * jnp.pi * phase.astype(F32) / NPHI
    return jnp.concatenate([jnp.cos(angles), -jnp.sin(angles)], axis=1).astype(BF16)


def local(spectra, legendre, pair_slots, theta_owner):
    lev, fields, slots, _, _ = spectra.shape
    ma, row = lax.axis_size("ma"), lax.axis_size("row")
    levels = lev * row
    half = legendre.shape[2]
    own = half // ma
    width = -(-own // LANES) * LANES
    share = -(-slots // row)
    extra = share * row - slots
    devices = ma * row
    synth_mat, analysis_mat = chebyshev_pair(levels)
    place = lax.axis_index("row")

    pairs = jnp.pad(pair_slots.reshape(ma, slots), ((0, 0), (0, extra)), constant_values=NPAIRS)
    mine = pairs.reshape(devices, share)[lax.axis_index("ma") * row + place]
    weights = slot_weights(mine)
    orders = jnp.stack([mine, LMAX - mine], axis=1)
    double = jnp.where(orders == 0, 1.0, 2.0).astype(F32)
    synth_weights = weights * double[:, :, None, None]

    every = pairs.reshape(devices * share)
    table = fourier_table(jnp.stack([every, LMAX - every], axis=1))
    table = table.reshape(devices, share * 4, NPHI)

    if extra:
        chosen = jnp.minimum(place * share + jnp.arange(share), slots - 1)
        functions = jnp.take(legendre, chosen, axis=0)
    else:
        functions = lax.dynamic_slice_in_dim(legendre, place * share, share, 0)
    owners = jnp.pad(
        theta_owner.reshape(ma, own), ((0, 0), (0, width - own)), constant_values=-1
    ).reshape(-1)
    order_rows = (jnp.arange(half)[:, None] == owners[None, :]).astype(BF16)
    functions = jnp.einsum(
        "sji,io->sjo", functions, order_rows, preferred_element_type=F32
    ).astype(BF16)

    outgoing = jnp.transpose(spectra, (2, 0, 1, 4, 3)).astype(BF16)
    outgoing = jnp.pad(outgoing, ((0, extra),) + ((0, 0),) * 4)
    incoming = lax.all_to_all(outgoing, "row", split_axis=0, concat_axis=0, tiled=True)
    incoming = incoming.reshape(row, share, lev, fields, 2, PACK).astype(F32)
    level_coeffs = jnp.einsum(
        "kzl,zslfcj->ksfcj", synth_mat.reshape(levels, row, lev), incoming, precision=HIGH
    ).astype(BF16)

    spread = jnp.transpose(level_coeffs, (1, 0, 2, 3, 4))[:, :, :, None, :, None, :]
    sel = jnp.transpose(synth_weights, (0, 2, 1, 3)).astype(BF16)[:, None, None, :, None, :, :]
    weighted = (spread * sel).reshape(share, levels * fields * 8, PACK)
    north_south = jnp.einsum(
        "smj,sjo->smo", weighted, functions, preferred_element_type=F32
    ).astype(BF16)
    north_south = north_south.reshape(share, row, lev, fields, 2, 4, ma, width)
    to_rows = jnp.transpose(north_south, (6, 1, 2, 3, 4, 0, 5, 7))
    to_rows = to_rows.reshape(devices, lev, fields, 2, share * 4, width)
    at_rows = lax.all_to_all(to_rows, ("ma", "row"), split_axis=0, concat_axis=0, tiled=True)

    grid = jnp.einsum("zlfhnr,znq->lfhrq", at_rows, table, preferred_element_type=F32)
    flux = (grid[:, 0:1] * grid[:, 1:3]).astype(BF16)
    fourier = jnp.einsum("znq,lghrq->zlghnr", table, flux, preferred_element_type=F32)
    fourier = (fourier * NPHI ** (-0.5)).astype(BF16)
    flux_grid = jnp.transpose(flux[:, :, :, :own], (0, 2, 3, 1, 4)).reshape(lev, 2 * own, 2, NPHI)
    back = lax.all_to_all(fourier, ("ma", "row"), split_axis=0, concat_axis=0, tiled=True)

    back = back.reshape(ma, row, lev, 2, 2, share, 2, 2, width)
    back = jnp.transpose(back, (0, 5, 7, 4, 1, 2, 3, 6, 8))
    back = back.reshape(ma, share, 4 * levels * 4, width)
    values = jnp.concatenate([back[d] for d in range(ma)], axis=-1)
    product = jnp.einsum("smo,sjo->smj", values, functions, preferred_element_type=F32)
    product = product.reshape(share, 4, levels * 4, PACK)
    spectral = jnp.sum(product * weights.reshape(share, 4, 1, PACK), axis=1)

    mix = jnp.kron(analysis_mat, jnp.eye(4, dtype=F32))
    mixed = jnp.einsum("nk,skj->nsj", mix, spectral, precision=HIGH).astype(BF16)
    mixed = mixed.reshape(row, lev, 2, 2, share, PACK)
    mixed = jnp.transpose(mixed, (0, 1, 2, 4, 3, 5))
    result = lax.all_to_all(mixed, "row", split_axis=0, concat_axis=0, tiled=True)
    result = jnp.transpose(result, (1, 2, 0, 3, 4, 5)).reshape(lev, 2, row * share, 2, PACK)
    flux_spectra = jnp.transpose(result[:, :, :slots], (0, 1, 2, 4, 3)).astype(F32)
    return (flux_grid, flux_spectra)


def solution(mesh):
    in_specs = (P("row", None, "ma", None, None), P("ma", None, None), P(), P())
    out_specs = (P("row", "ma", None, None), P("row", None, "ma", None, None))
    return jax.shard_map(local, mesh=mesh, in_specs=in_specs, out_specs=out_specs, check_vma=False)
```

```python
import jax
import jax.numpy as jnp
from jax import lax
from jax.sharding import PartitionSpec as P

LMAX = 511
NPHI = 1536
NPAIRS = 256
PACK = 513

HIGH = lax.Precision.HIGHEST
BF16 = jnp.bfloat16
F32 = jnp.float32


def chebyshev_pair(levels):
    index = jnp.arange(levels, dtype=jnp.int32)
    products = index[:, None] * index[None, :] % (2 * (levels - 1))
    cosines = jnp.cos(jnp.pi * products.astype(F32) / (levels - 1))
    ends = jnp.where((index == 0) | (index == levels - 1), 0.5, 1.0).astype(F32)
    analysis = (2.0 / (levels - 1)) ** 0.5 * ends[:, None] * ends[None, :] * cosines
    return (cosines, analysis)


def slot_weights(pairs):
    packed = jnp.arange(PACK, dtype=jnp.int32)[None, :]
    column = pairs[:, None]
    in_use = column < NPAIRS
    low = (in_use & (packed <= LMAX - column)).astype(F32)
    high = (in_use & (packed > LMAX - column)).astype(F32)
    low_sign = (1 - 2 * (packed % 2)).astype(F32)
    high_sign = (1 - 2 * ((packed + LMAX - column + 1) % 2)).astype(F32)
    return jnp.stack(
        [jnp.stack([low, low * low_sign], 1), jnp.stack([high, high * high_sign], 1)], 1
    )


def fourier_table(orders):
    points = jnp.arange(NPHI, dtype=jnp.int32)
    phase = orders[:, None, :, None] * points % NPHI
    angles = 2.0 * jnp.pi * phase.astype(F32) / NPHI
    return jnp.concatenate([jnp.cos(angles), -jnp.sin(angles)], axis=1).astype(BF16)


def local(spectra, legendre, pair_slots, theta_owner):
    lev, fields, slots, _, _ = spectra.shape
    ma, row = lax.axis_size("ma"), lax.axis_size("row")
    levels = lev * row
    half = legendre.shape[2]
    own = half // ma
    share = -(-slots // row)
    extra = share * row - slots
    devices = ma * row
    synth_mat, analysis_mat = chebyshev_pair(levels)
    place = lax.axis_index("row")

    pairs = jnp.pad(pair_slots.reshape(ma, slots), ((0, 0), (0, extra)), constant_values=NPAIRS)
    mine = pairs.reshape(devices, share)[lax.axis_index("ma") * row + place]
    weights = slot_weights(mine)
    orders = jnp.stack([mine, LMAX - mine], axis=1)
    double = jnp.where(orders == 0, 1.0, 2.0).astype(F32)
    synth_weights = weights * double[:, :, None, None]

    every = pairs.reshape(devices * share)
    table = fourier_table(jnp.stack([every, LMAX - every], axis=1))
    table = table.reshape(devices, share * 4, NPHI)

    if extra:
        chosen = jnp.minimum(place * share + jnp.arange(share), slots - 1)
        functions = jnp.take(legendre, chosen, axis=0)
    else:
        functions = lax.dynamic_slice_in_dim(legendre, place * share, share, 0)
    order_rows = (jnp.arange(half)[:, None] == theta_owner[None, :]).astype(BF16)
    functions = jnp.einsum(
        "sji,io->sjo", functions, order_rows, preferred_element_type=F32
    ).astype(BF16)

    outgoing = jnp.transpose(spectra, (2, 0, 1, 4, 3)).astype(BF16)
    outgoing = jnp.pad(outgoing, ((0, extra),) + ((0, 0),) * 4)
    incoming = lax.all_to_all(outgoing, "row", split_axis=0, concat_axis=0, tiled=True)
    incoming = incoming.reshape(row, share, lev, fields, 2, PACK).astype(F32)
    level_coeffs = jnp.einsum(
        "kzl,zslfcj->ksfcj", synth_mat.reshape(levels, row, lev), incoming, precision=HIGH
    ).astype(BF16)

    spread = jnp.transpose(level_coeffs, (1, 2, 0, 3, 4))[:, :, None, :, :, None, :]
    sel = jnp.transpose(synth_weights, (0, 2, 1, 3)).astype(BF16)[:, None, :, None, None, :, :]
    weighted = (spread * sel).reshape(share, fields * 2 * levels * 4, PACK)
    north_south = jnp.einsum(
        "smj,sjo->smo", weighted, functions, preferred_element_type=F32
    ).astype(BF16)
    north_south = north_south.reshape(share, fields * 2, row, lev, 4, half)
    to_rows = [
        jnp.concatenate(
            [north_south[:, x, ..., d * own : (d + 1) * own] for x in range(fields * 2)], axis=-1
        )
        for d in range(ma)
    ]
    to_rows = jnp.transpose(jnp.stack(to_rows), (0, 2, 3, 1, 4, 5))
    to_rows = to_rows.reshape(devices, lev, share * 4, fields * 2 * own)
    at_rows = lax.all_to_all(to_rows, ("ma", "row"), split_axis=0, concat_axis=0, tiled=True)

    grid = jnp.einsum("zlnm,znq->lmq", at_rows, table, preferred_element_type=F32)
    grid = grid.reshape(lev, fields, 2 * own, NPHI)
    flux = (grid[:, 0:1] * grid[:, 1:3]).astype(BF16)
    fourier = jnp.einsum(
        "znq,lmq->zlnm", table, flux.reshape(lev, 4 * own, NPHI), preferred_element_type=F32
    )
    fourier = (fourier * NPHI ** (-0.5)).astype(BF16)
    flux_grid = jnp.transpose(flux, (0, 2, 1, 3))
    back = lax.all_to_all(fourier, ("ma", "row"), split_axis=0, concat_axis=0, tiled=True)

    back = back.reshape(ma, row, lev, share, 2, 2, 4 * own)
    values = [
        jnp.concatenate([back[d, ..., x * own : (x + 1) * own] for d in range(ma)], axis=-1)
        for x in range(4)
    ]
    values = jnp.stack(values).reshape(2, 2, row, lev, share, 2, 2, half)
    values = jnp.transpose(values, (4, 6, 1, 2, 3, 0, 5, 7))
    values = values.reshape(share, 4 * levels * 4, half)
    product = jnp.einsum("smo,sjo->smj", values, functions, preferred_element_type=F32)
    product = product.reshape(share, 4, levels * 4, PACK)
    spectral = jnp.sum(product * weights.reshape(share, 4, 1, PACK), axis=1)

    mix = jnp.kron(analysis_mat, jnp.eye(4, dtype=F32))
    mixed = jnp.einsum("nk,skj->nsj", mix, spectral, precision=HIGH).astype(BF16)
    mixed = mixed.reshape(row, lev, 2, 2, share, PACK)
    mixed = jnp.transpose(mixed, (0, 1, 2, 4, 3, 5))
    result = lax.all_to_all(mixed, "row", split_axis=0, concat_axis=0, tiled=True)
    result = jnp.transpose(result, (1, 2, 0, 3, 4, 5)).reshape(lev, 2, row * share, 2, PACK)
    flux_spectra = jnp.transpose(result[:, :, :slots], (0, 1, 2, 4, 3)).astype(F32)
    return (flux_grid, flux_spectra)


def solution(mesh):
    in_specs = (P("row", None, "ma", None, None), P("ma", None, None), P(), P())
    out_specs = (P("row", "ma", None, None), P("row", None, "ma", None, None))
    return jax.shard_map(local, mesh=mesh, in_specs=in_specs, out_specs=out_specs, check_vma=False)
```

```python
import jax
import jax.numpy as jnp
from jax import lax
from jax.sharding import PartitionSpec as P

LMAX = 511
NPHI = 1536
NPAIRS = 256
PACK = 513
LANES = 128

HIGH = lax.Precision.HIGHEST
BF16 = jnp.bfloat16
F32 = jnp.float32


def chebyshev_pair(levels):
    index = jnp.arange(levels, dtype=jnp.int32)
    products = index[:, None] * index[None, :] % (2 * (levels - 1))
    cosines = jnp.cos(jnp.pi * products.astype(F32) / (levels - 1))
    ends = jnp.where((index == 0) | (index == levels - 1), 0.5, 1.0).astype(F32)
    analysis = (2.0 / (levels - 1)) ** 0.5 * ends[:, None] * ends[None, :] * cosines
    return (cosines, analysis)


def slot_weights(pairs):
    packed = jnp.arange(PACK, dtype=jnp.int32)[None, :]
    column = pairs[:, None]
    in_use = column < NPAIRS
    low = (in_use & (packed <= LMAX - column)).astype(F32)
    high = (in_use & (packed > LMAX - column)).astype(F32)
    low_sign = (1 - 2 * (packed % 2)).astype(F32)
    high_sign = (1 - 2 * ((packed + LMAX - column + 1) % 2)).astype(F32)
    return jnp.stack(
        [jnp.stack([low, low * low_sign], 1), jnp.stack([high, high * high_sign], 1)], 1
    )


def fourier_table(orders):
    points = jnp.arange(NPHI, dtype=jnp.int32)
    phase = orders[:, None, :, None] * points % NPHI
    angles = 2.0 * jnp.pi * phase.astype(F32) / NPHI
    return jnp.concatenate([jnp.cos(angles), -jnp.sin(angles)], axis=1).astype(BF16)


def local(spectra, legendre, pair_slots, theta_owner):
    lev, fields, slots, _, _ = spectra.shape
    ma, row = lax.axis_size("ma"), lax.axis_size("row")
    levels = lev * row
    half = legendre.shape[2]
    own = half // ma
    width = -(-own // LANES) * LANES
    share = -(-slots // row)
    extra = share * row - slots
    devices = ma * row
    synth_mat, analysis_mat = chebyshev_pair(levels)
    place = lax.axis_index("row")

    pairs = jnp.pad(pair_slots.reshape(ma, slots), ((0, 0), (0, extra)), constant_values=NPAIRS)
    mine = pairs.reshape(devices, share)[lax.axis_index("ma") * row + place]
    weights = slot_weights(mine)
    orders = jnp.stack([mine, LMAX - mine], axis=1)
    double = jnp.where(orders == 0, 1.0, 2.0).astype(F32)
    synth_weights = weights * double[:, :, None, None]

    every = pairs.reshape(devices * share)
    table = fourier_table(jnp.stack([every, LMAX - every], axis=1))
    table = table.reshape(devices, share * 4, NPHI)

    if extra:
        chosen = jnp.minimum(place * share + jnp.arange(share), slots - 1)
        functions = jnp.take(legendre, chosen, axis=0)
    else:
        functions = lax.dynamic_slice_in_dim(legendre, place * share, share, 0)
    owners = jnp.pad(
        theta_owner.reshape(ma, own), ((0, 0), (0, width - own)), constant_values=-1
    ).reshape(-1)
    order_rows = (jnp.arange(half)[:, None] == owners[None, :]).astype(BF16)
    functions = jnp.einsum(
        "sji,io->sjo", functions, order_rows, preferred_element_type=F32
    ).astype(BF16)

    outgoing = jnp.transpose(spectra, (2, 0, 1, 4, 3)).astype(BF16)
    outgoing = jnp.pad(outgoing, ((0, extra),) + ((0, 0),) * 4)
    incoming = lax.all_to_all(outgoing, "row", split_axis=0, concat_axis=0, tiled=True)
    incoming = incoming.reshape(row, share, lev, fields, 2, PACK).astype(F32)
    level_coeffs = jnp.einsum(
        "kzl,zslfcj->ksfcj", synth_mat.reshape(levels, row, lev), incoming, precision=HIGH
    ).astype(BF16)

    spread = jnp.transpose(level_coeffs, (1, 0, 2, 3, 4))[:, :, :, None, :, None, :]
    sel = jnp.transpose(synth_weights, (0, 2, 1, 3)).astype(BF16)[:, None, None, :, None, :, :]
    weighted = (spread * sel).reshape(share, levels * fields * 8, PACK)
    north_south = jnp.einsum(
        "smj,sjo->smo", weighted, functions, preferred_element_type=F32
    ).astype(BF16)
    north_south = north_south.reshape(share, row, lev, fields, 2, 4, ma, width)
    to_rows = jnp.transpose(north_south, (6, 1, 2, 3, 4, 0, 5, 7))
    to_rows = to_rows.reshape(devices, lev, fields, 2, share * 4, width)
    at_rows = lax.all_to_all(to_rows, ("ma", "row"), split_axis=0, concat_axis=0, tiled=True)

    def on_grid(values):
        return jnp.einsum("zlfhnr,znq->lfhrq", values, table, preferred_element_type=F32)

    first = on_grid(at_rows[:, :, 0:2])
    velocity = first[:, 0]
    scalars = (first[:, 1], on_grid(at_rows[:, :, 2:3])[:, 0])
    fluxes, parts = [], []
    for scalar in scalars:
        flux = (velocity * scalar).astype(BF16)
        fluxes.append(flux)
        fourier = jnp.einsum("znq,lhrq->zlhnr", table, flux, preferred_element_type=F32)
        fourier = (fourier * NPHI ** (-0.5)).astype(BF16)
        back = lax.all_to_all(fourier, ("ma", "row"), split_axis=0, concat_axis=0, tiled=True)

        back = back.reshape(ma, row, lev, 2, share, 2, 2, width)
        back = jnp.transpose(back, (0, 4, 6, 3, 1, 2, 5, 7))
        back = back.reshape(ma, share, 4 * levels * 2, width)
        values = jnp.concatenate([back[d] for d in range(ma)], axis=-1)
        product = jnp.einsum("smo,sjo->smj", values, functions, preferred_element_type=F32)
        product = product.reshape(share, 4, levels * 2, PACK)
        parts.append(jnp.sum(product * weights.reshape(share, 4, 1, PACK), axis=1))
    flux_grid = jnp.stack([flux[:, :, :own] for flux in fluxes], axis=3)
    flux_grid = flux_grid.reshape(lev, 2 * own, 2, NPHI)

    mix = jnp.kron(analysis_mat, jnp.eye(2, dtype=F32))
    mixed = [
        jnp.einsum("nk,skj->nsj", mix, part, precision=HIGH)
        .astype(BF16)
        .reshape(row, lev, 2, share, PACK)
        for part in parts
    ]
    mixed = jnp.transpose(jnp.stack(mixed, axis=2), (0, 1, 2, 4, 3, 5))
    result = lax.all_to_all(mixed, "row", split_axis=0, concat_axis=0, tiled=True)
    result = jnp.transpose(result, (1, 2, 0, 3, 4, 5)).reshape(lev, 2, row * share, 2, PACK)
    flux_spectra = jnp.transpose(result[:, :, :slots], (0, 1, 2, 4, 3)).astype(F32)
    return (flux_grid, flux_spectra)


def solution(mesh):
    in_specs = (P("row", None, "ma", None, None), P("ma", None, None), P(), P())
    out_specs = (P("row", "ma", None, None), P("row", None, "ma", None, None))
    return jax.shard_map(local, mesh=mesh, in_specs=in_specs, out_specs=out_specs, check_vma=False)
```
